256 devices in a mesh: pipe: 8 (over x, core), graph: 32 (over y, z).
Axes of the slice: x: 4, y: 4, z: 8, core: 2. Of those that a mesh axis runs over, the one named last changes fastest.
Arguments:
- features: bfloat16 [4, 8192, 1024], P(None, 'graph'), may hold values from -6 to 6
- weights: bfloat16 [8, 1024, 1024], P('pipe'), may hold values from -0.1875 to 0.1875
- gains: float32 [8, 1024], P('pipe'), may hold values from 0.5 to 1.5
- tiles: bfloat16 [4, 384, 128, 128], P(None, 'graph'), may hold values from 0 to 0.16764323, as said below
- tile_coords: int32 [4, 384, 2], P(None, 'graph'), may hold values from 0 to 3, as said below
- send_ids: int32 [4, 32, 2, 1], replicated, may hold values from 0 to 1
Outputs:
- activations: bfloat16 [8, 4, 8192, 1024], P('pipe', None, 'graph')
The draws below stay inside these ranges and needn't reach their ends.
Inputs may be any that keep to these rules, and one draw needn't show every extreme that they name: `tile_coords`: each row is (destination block, source slot): slots below 2 are the partition's own blocks, the next 1 come from the partition before, the last 1 from the partition after; in every micro-batch and partition every slot and every destination block is named by some tile. `tiles`: nonnegative adjacency weights.
All inputs are finite; a program needn't handle non-finite values.
Results may differ from the reference program's by a relative error of at most 0.0085.
Values may be sent and summed in bfloat16 or wider, within the bound.
A program may use at most 64 MiB of HBM per device.

```python
import jax
import jax.numpy as jnp
from jax import lax

H = 1024
TILE = 128
BLOCKS = 2
SENDS = 1
TILE_ROW = 6
MB = 4
LAYERS = 8
PARTITIONS = 32
TILES_DEV = 12
TILES = 384
NODES = 8192


def draw_tile_coords(key, part):
    key = jax.random.fold_in(key, 11)
    key_a, key_b, key_c, key_d = jax.random.split(key, 4)
    slots = BLOCKS + 2 * SENDS
    groups = TILES // TILES_DEV
    position = jnp.arange(TILES_DEV, dtype=jnp.int32)[None, None, :]
    shift_src = jax.random.randint(key_a, (MB, groups, 1), 0, slots, dtype=jnp.int32)
    shift_dst = jax.random.randint(key_b, (MB, groups, 1), 0, BLOCKS, dtype=jnp.int32)
    loose_src = jax.random.randint(key_c, (MB, groups, TILES_DEV), 0, slots, dtype=jnp.int32)
    loose_dst = jax.random.randint(key_d, (MB, groups, TILES_DEV), 0, BLOCKS, dtype=jnp.int32)
    source = jnp.where(position < slots, (position + shift_src) % slots, loose_src)
    target = jnp.where(position < BLOCKS, (position + shift_dst) % BLOCKS, loose_dst)
    both = jnp.stack([target, source], axis=-1)
    return both.reshape(MB, TILES, 2).astype(jnp.int32)


def sparse_tiles(key, main_lo, extra_rate, extra_lo):
    key_a, key_b, key_c, key_d, key_e = jax.random.split(key, 5)
    factor = 2 * jax.random.randint(key_a, (MB, TILES, 1, 1), 0, TILE // 2, dtype=jnp.int32) + 1
    offset = jax.random.randint(key_b, (MB, TILES, 1, 1), 0, TILE, dtype=jnp.int32)
    rows = jnp.arange(TILE, dtype=jnp.int32)[None, None, :, None]
    cols = jnp.arange(TILE, dtype=jnp.int32)[None, None, None, :]
    on_main = (rows * factor + offset) % TILE == cols
    main_value = jax.random.uniform(key_c, (MB, TILES, TILE, TILE), jnp.float32, main_lo, 1.0)
    extra_on = jax.random.uniform(key_d, (MB, TILES, TILE, TILE), jnp.float32) < extra_rate
    extra_value = jax.random.uniform(key_e, (MB, TILES, TILE, TILE), jnp.float32, extra_lo, 1.0)
    entry = jnp.where(on_main, main_value, jnp.where(extra_on, extra_value, 0.0))
    return (entry / TILE_ROW).astype(jnp.bfloat16)


def draw_tiles(key, part):
    key = jax.random.fold_in(key, 23)
    return sparse_tiles(key, 0.5, 2.0 / TILE, 0.0)


def set_ends(result, own_key, smallest, top_value):
    index_at = [jax.random.randint(jax.random.fold_in(own_key, axis), (), 0, length) for axis, length in enumerate(result.shape)]
    widest = result.shape.index(max(result.shape))
    next_to = index_at[:widest] + [(index_at[widest] + 1) % result.shape[widest]] + index_at[widest + 1:]
    return result.at[tuple(index_at)].set(smallest).at[tuple(next_to)].set(top_value)


def levels(key, shape, cuts, least, high):
    level, own = 1.0, jax.random.fold_in(key, 6)
    for dim, shards_of in cuts:
        steps = jnp.exp(jax.random.uniform(jax.random.fold_in(own, dim), (shards_of,), jnp.float32, least / len(cuts), high / len(cuts)))
        level = level * jnp.repeat(steps, shape[dim] // shards_of).reshape([-1 if axis == dim else 1 for axis in range(len(shape))])
    return level


def normal_values(rng, extent, deviation, reach, cuts=(), kind=jnp.bfloat16):
    values = jax.random.normal(rng, extent, jnp.float32) * deviation
    if len(cuts) > 0:
        values = levels(rng, extent, cuts, -0.22, 0.18) * values
    return jnp.clip(values, min=-reach, max=reach).astype(kind)


def setup_inputs(seed: int = 0) -> dict:
    streams_of = jax.random.split(jax.random.key(seed), 7)
    return {
        "features": normal_values(streams_of[0], (MB, NODES, H), 1.0, 6.0, ((1, 32),)),
        "weights": normal_values(streams_of[1], (LAYERS, H, H), H ** -0.5, 0.1875, ((0, 8),)),
        "gains": jnp.clip(1.0 + 0.1 * jax.random.normal(streams_of[2], (LAYERS, H), jnp.float32), 0.5, 1.5),
        "tiles": draw_tiles(jax.random.fold_in(streams_of[6], 71), 0),
        "tile_coords": draw_tile_coords(jax.random.fold_in(streams_of[6], 71), 0),
        "send_ids": set_ends(jax.random.randint(streams_of[5], (MB, PARTITIONS, 2, SENDS), 0, BLOCKS), jax.random.fold_in(streams_of[5], 1), 0, BLOCKS - 1).astype(jnp.int32),
    }


def part_layer(blocked, from_left, from_right, tile, coords, weight, gain):
    nblocks = blocked.shape[0]
    edge = blocked.shape[1]
    width = blocked.shape[2]
    count = tile.shape[0]
    sources = jnp.concatenate([blocked, from_left, from_right], axis=0)
    slots = sources.shape[0]
    dest_hot = (coords[:, 0][:, None] == jnp.arange(nblocks, dtype=jnp.int32)[None, :]).astype(jnp.float32)
    slot_hot = (coords[:, 1][:, None] == jnp.arange(slots, dtype=jnp.int32)[None, :]).astype(jnp.float32)
    pairing = (dest_hot[:, :, None] * slot_hot[:, None, :]).reshape(count, nblocks * slots)
    flat_tiles = tile.astype(jnp.float32).reshape(count, edge * edge)
    table = jnp.dot(pairing.T, flat_tiles, precision=lax.Precision.HIGHEST)
    table = table.reshape(nblocks, slots, edge, edge)
    table = jnp.transpose(table, (0, 2, 1, 3)).reshape(nblocks * edge, slots * edge).astype(jnp.bfloat16)
    agg = jnp.dot(table, sources.reshape(slots * edge, width), preferred_element_type=jnp.float32).astype(jnp.bfloat16)
    z = jnp.dot(agg, weight, preferred_element_type=jnp.float32)
    act = jnp.maximum(z, 0.0)
    scale = 1.0 / jnp.sqrt(lax.optimization_barrier(jnp.mean(act * act, axis=-1, keepdims=True)) + 1e-06)
    return (act * scale * gain[None, :]).astype(jnp.bfloat16)

def reference(features, weights, gains, tiles, tile_coords, send_ids):
    layers_out = []
    for layer in range(LAYERS):
        layers_out.append([])
    for micro in range(MB):
        current = features[micro].reshape(PARTITIONS, BLOCKS, TILE, H)
        tile_m = tiles[micro].reshape(PARTITIONS, TILES_DEV, TILE, TILE)
        coord_m = tile_coords[micro].reshape(PARTITIONS, TILES_DEV, 2)
        ids = send_ids[micro]
        for layer in range(LAYERS):
            left = jnp.roll(current, 1, axis=0)
            left_ids = jnp.roll(ids[:, 0], 1, axis=0)
            right = jnp.roll(current, -1, axis=0)
            right_ids = jnp.roll(ids[:, 1], -1, axis=0)
            from_left = jax.vmap(lambda block_set, picks: block_set[picks])(left, left_ids)
            from_right = jax.vmap(lambda block_set, picks: block_set[picks])(right, right_ids)
            fresh = jax.vmap(part_layer, in_axes=(0, 0, 0, 0, 0, None, None))(current, from_left, from_right, tile_m, coord_m, weights[layer], gains[layer])
            layers_out[layer].append(fresh.reshape(NODES, H))
            current = fresh.reshape(PARTITIONS, BLOCKS, TILE, H)
    return jnp.stack([jnp.stack(group, axis=0) for group in layers_out], axis=0)
```

```python
import functools

import jax
import jax.numpy as jnp
from jax import lax
from jax.experimental import pallas as pl
from jax.experimental.pallas import tpu as pltpu
from jax.sharding import PartitionSpec as P

MESH = pl.DeviceIdType.MESH
CHUNKS = 4


def kernel(
    sections,
    partitions,
    ids_ref,
    coords_ref,
    gain_ref,
    features_ref,
    weight_hbm,
    tiles_hbm,
    out_hbm,
    own,
    halo,
    fwd_stage,
    halo_stage,
    result,
    weight,
    tiles,
    table,
    z_acc,
    own_send,
    own_recv,
    fwd_send,
    halo_send,
    halo_recv,
    feature_sem,
    out_sem,
    load_sem,
):
    p = lax.axis_index("pipe")
    g = lax.axis_index("graph")
    right = lax.rem(g + 1, partitions)
    left = lax.rem(g + partitions - 1, partitions)
    micro_count, chunks, rows, cols = own.shape
    edge = halo.shape[3]
    tile_count = tiles.shape[1]
    slots = rows // edge + 2
    even = lax.rem(p, 2) == 0
    odd = jnp.logical_not(even)
    first = p == 0
    has_next = p < sections - 1
    ahead = jnp.minimum(p + 1, sections - 1)
    behind = jnp.maximum(p - 1, 0)

    load_weight = pltpu.make_async_copy(weight_hbm, weight, load_sem.at[0])
    load_tiles = pltpu.make_async_copy(tiles_hbm, tiles, load_sem.at[1])

    def load_features(m, c):
        return pltpu.make_async_copy(
            features_ref.at[m, :, pl.ds(c * cols, cols)], own.at[m, c], feature_sem.at[m, c]
        )

    def send_own(m, c):
        return pltpu.make_async_remote_copy(
            src_ref=result.at[m, c],
            dst_ref=own.at[m, c],
            send_sem=own_send.at[m, c],
            recv_sem=own_recv.at[m, c],
            device_id=(ahead, g),
            device_id_type=MESH,
        )

    def send_forward(m, side, c):
        return pltpu.make_async_remote_copy(
            src_ref=fwd_stage.at[m, side, c],
            dst_ref=halo.at[m, side, c],
            send_sem=fwd_send.at[m, side, c],
            recv_sem=halo_recv.at[m, side, c],
            device_id=(p, left if side else right),
            device_id_type=MESH,
        )

    def send_halo(m, side, c):
        return pltpu.make_async_remote_copy(
            src_ref=halo_stage.at[m, side, c],
            dst_ref=halo.at[m, side, c],
            send_sem=halo_send.at[m, side, c],
            recv_sem=halo_recv.at[m, side, c],
            device_id=(ahead, left if side else right),
            device_id_type=MESH,
        )

    def save(m, c):
        return pltpu.make_async_copy(
            result.at[m, c], out_hbm.at[m, :, pl.ds(c * cols, cols)], out_sem.at[m, c]
        )

    load_tiles.start()
    load_weight.start()

    @pl.when(first)
    def _():
        for m in range(micro_count):
            for c in range(chunks):
                load_features(m, c).start()

    barrier = pltpu.get_barrier_semaphore()

    def greet(*where):
        for device in where:
            pl.semaphore_signal(barrier, inc=1, device_id=device, device_id_type=MESH)

    @pl.when(even)
    def _():
        greet((p, right), (p, left), (ahead, g), (ahead, right), (ahead, left))

    @pl.when(odd)
    def _():
        greet((behind, g), (behind, right), (behind, left))

    @pl.when(jnp.logical_and(even, p > 0))
    def _():
        greet((behind, g))

    @pl.when(jnp.logical_and(odd, has_next))
    def _():
        greet((ahead, g))

    @pl.when(first)
    def _():
        pl.semaphore_wait(barrier, 5)

    @pl.when(jnp.logical_and(even, p > 0))
    def _():
        pl.semaphore_wait(barrier, 6)

    @pl.when(jnp.logical_and(odd, has_next))
    def _():
        pl.semaphore_wait(barrier, 4)

    @pl.when(p == sections - 1)
    def _():
        pl.semaphore_wait(barrier, 3)

    def picked(block, m, side):
        chosen = ids_ref[m, g, side, 0]
        return jnp.where(chosen == 0, block[:edge], block[edge:])

    def forward(m):
        for c in range(chunks):

            @pl.when(first)
            def _():
                load_features(m, c).wait()

            @pl.when(p > 0)
            def _():
                send_own(m, c).wait_recv()

            block = own[m, c]
            for side in range(2):
                fwd_stage[m, side, c] = picked(block, m, side)
                send_forward(m, side, c).start()

    @pl.when(first)
    def _():
        forward(0)

    load_tiles.wait()

    def build_table(m, carry):
        for d in range(rows // edge):
            for s in range(slots):
                total = jnp.zeros((edge, edge), jnp.float32)
                for t in range(tile_count):
                    here = jnp.logical_and(coords_ref[m, t, 0] == d, coords_ref[m, t, 1] == s)
                    total += tiles[m, t].astype(jnp.float32) * jnp.where(here, 1.0, 0.0)
                table[m, pl.ds(d * edge, edge), pl.ds(s * edge, edge)] = total.astype(jnp.bfloat16)
        return carry

    lax.fori_loop(0, micro_count, build_table, 0)
    load_weight.wait()

    def micro_step(m, carry):
        @pl.when(jnp.logical_and(even, jnp.logical_or(p > 0, m > 0)))
        def _():
            forward(m)

        for c in range(chunks):

            @pl.when(odd)
            def _():
                send_own(m, c).wait_recv()

            agg = jnp.dot(
                table[m, :, :rows], own[m, c], preferred_element_type=jnp.float32
            )
            for side in range(2):
                send_forward(m, side, c).wait_recv()
                agg += jnp.dot(
                    table[m, :, pl.ds(rows + side * edge, edge)],
                    halo[m, side, c],
                    preferred_element_type=jnp.float32,
                )
            part = jnp.dot(
                agg.astype(jnp.bfloat16),
                weight[pl.ds(c * cols, cols), :],
                preferred_element_type=jnp.float32,
            )
            if c == 0:
                z_acc[...] = part
            elif c < chunks - 1:
                z_acc[...] += part
            else:
                act = jnp.maximum(z_acc[...] + part, 0.0)
        scale = 1.0 / jnp.sqrt(jnp.mean(act * act, axis=-1, keepdims=True) + 1e-06)
        for c in range(chunks):
            block = act[:, c * cols : (c + 1) * cols] * scale
            block = (block * gain_ref[:, pl.ds(c * cols, cols)]).astype(jnp.bfloat16)
            result[m, c] = block

            @pl.when(even)
            def _():
                for side in range(2):
                    halo_stage[m, side, c] = picked(block, m, side)
                    send_halo(m, side, c).start()

            @pl.when(has_next)
            def _():
                send_own(m, c).start()

            save(m, c).start()
        return carry

    lax.fori_loop(0, micro_count, micro_step, 0)

    def finish(m, carry):
        for c in range(chunks):
            save(m, c).wait()

            @pl.when(has_next)
            def _():
                send_own(m, c).wait_send()

            @pl.when(even)
            def _():
                for side in range(2):
                    send_forward(m, side, c).wait_send()
                    send_halo(m, side, c).wait_send()

        return carry

    lax.fori_loop(0, micro_count, finish, 0)


def on_device(features, weights, gains, tiles, tile_coords, send_ids):
    micro_count, rows, width = features.shape
    tile_count, edge = tiles.shape[1], tiles.shape[-1]
    slots = rows // edge + 2
    cols = width // CHUNKS
    per_chunk = (micro_count, CHUNKS)
    per_side = (micro_count, 2, CHUNKS)
    result = pl.pallas_call(
        functools.partial(kernel, lax.axis_size("pipe"), lax.axis_size("graph")),
        out_shape=jax.ShapeDtypeStruct((micro_count, rows, width), jnp.bfloat16),
        in_specs=[
            pl.BlockSpec(memory_space=pltpu.SMEM),
            pl.BlockSpec(memory_space=pltpu.SMEM),
            pl.BlockSpec(memory_space=pltpu.VMEM),
            pl.BlockSpec(memory_space=pl.ANY),
            pl.BlockSpec(memory_space=pl.ANY),
            pl.BlockSpec(memory_space=pl.ANY),
        ],
        out_specs=pl.BlockSpec(memory_space=pl.ANY),
        scratch_shapes=[
            pltpu.VMEM(per_chunk + (rows, cols), jnp.bfloat16),
            pltpu.VMEM(per_side + (edge, cols), jnp.bfloat16),
            pltpu.VMEM(per_side + (edge, cols), jnp.bfloat16),
            pltpu.VMEM(per_side + (edge, cols), jnp.bfloat16),
            pltpu.VMEM(per_chunk + (rows, cols), jnp.bfloat16),
            pltpu.VMEM((width, width), jnp.bfloat16),
            pltpu.VMEM((micro_count, tile_count, edge, edge), jnp.bfloat16),
            pltpu.VMEM((micro_count, rows, slots * edge), jnp.bfloat16),
            pltpu.VMEM((rows, width), jnp.float32),
            pltpu.SemaphoreType.DMA(per_chunk),
            pltpu.SemaphoreType.DMA(per_chunk),
            pltpu.SemaphoreType.DMA(per_side),
            pltpu.SemaphoreType.DMA(per_side),
            pltpu.SemaphoreType.DMA(per_side),
            pltpu.SemaphoreType.DMA(per_chunk),
            pltpu.SemaphoreType.DMA(per_chunk),
            pltpu.SemaphoreType.DMA((2,)),
        ],
        compiler_params=pltpu.CompilerParams(
            collective_id=0, has_side_effects=True, vmem_limit_bytes=48 * 1024 * 1024
        ),
    )(send_ids, tile_coords, gains, features, weights[0], tiles)
    return result[None]


def solution(mesh):
    placed = (
        P(None, "graph", None),
        P("pipe", None, None),
        P("pipe", None),
        P(None, "graph", None, None),
        P(None, "graph", None),
        P(),
    )
    return jax.shard_map(
        on_device,
        mesh=mesh,
        in_specs=placed,
        out_specs=P("pipe", None, "graph", None),
        check_vma=False,
    )
```

```python
import functools

import jax
import jax.numpy as jnp
from jax import lax
from jax.experimental import pallas as pl
from jax.experimental.pallas import tpu as pltpu
from jax.sharding import PartitionSpec as P

MESH = pl.DeviceIdType.MESH
CHUNKS = 4


def kernel(
    sections,
    partitions,
    ids_ref,
    coords_ref,
    gain_hbm,
    features_ref,
    weight_hbm,
    tiles_hbm,
    out_hbm,
    own,
    halo,
    fwd_stage,
    halo_stage,
    result,
    weight,
    gain_ref,
    tiles,
    table,
    z_acc,
    own_send,
    own_recv,
    fwd_send,
    halo_send,
    halo_recv,
    feature_sem,
    out_sem,
    load_sem,
):
    p = lax.axis_index("pipe")
    g = lax.axis_index("graph")
    right = lax.rem(g + 1, partitions)
    left = lax.rem(g + partitions - 1, partitions)
    micro_count, chunks, rows, cols = own.shape
    edge = halo.shape[3]
    tile_count = tiles.shape[1]
    slots = rows // edge + 2
    even = lax.rem(p, 2) == 0
    odd = jnp.logical_not(even)
    first = p == 0
    has_next = p < sections - 1
    ahead = jnp.minimum(p + 1, sections - 1)
    behind = jnp.maximum(p - 1, 0)

    load_weight = pltpu.make_async_copy(weight_hbm, weight, load_sem.at[0])
    load_gain = pltpu.make_async_copy(gain_hbm, gain_ref, load_sem.at[2])
    load_tiles = pltpu.make_async_copy(tiles_hbm, tiles, load_sem.at[1])

    def load_features(m, c):
        return pltpu.make_async_copy(
            features_ref.at[m, :, pl.ds(c * cols, cols)], own.at[m, c], feature_sem.at[m, c]
        )

    def send_own(m, c):
        return pltpu.make_async_remote_copy(
            src_ref=result.at[m, c],
            dst_ref=own.at[m, c],
            send_sem=own_send.at[m, c],
            recv_sem=own_recv.at[m, c],
            device_id=(ahead, g),
            device_id_type=MESH,
        )

    def send_forward(m, side, c):
        return pltpu.make_async_remote_copy(
            src_ref=fwd_stage.at[m, side, c],
            dst_ref=halo.at[m, side, c],
            send_sem=fwd_send.at[m, side, c],
            recv_sem=halo_recv.at[m, side, c],
            device_id=(p, left if side else right),
            device_id_type=MESH,
        )

    def send_halo(m, side, c):
        return pltpu.make_async_remote_copy(
            src_ref=halo_stage.at[m, side, c],
            dst_ref=halo.at[m, side, c],
            send_sem=halo_send.at[m, side, c],
            recv_sem=halo_recv.at[m, side, c],
            device_id=(ahead, left if side else right),
            device_id_type=MESH,
        )

    def save(m, c):
        return pltpu.make_async_copy(
            result.at[m, c], out_hbm.at[m, :, pl.ds(c * cols, cols)], out_sem.at[m, c]
        )

    load_tiles.start()
    load_weight.start()
    load_gain.start()

    @pl.when(first)
    def _():
        for m in range(micro_count):
            for c in range(chunks):
                load_features(m, c).start()

    barrier = pltpu.get_barrier_semaphore()

    def greet(*where):
        for device in where:
            pl.semaphore_signal(barrier, inc=1, device_id=device, device_id_type=MESH)

    @pl.when(even)
    def _():
        greet((p, right), (p, left), (ahead, g), (ahead, right), (ahead, left))

    @pl.when(odd)
    def _():
        greet((behind, g), (behind, right), (behind, left))

    @pl.when(jnp.logical_and(even, p > 0))
    def _():
        greet((behind, g))

    @pl.when(jnp.logical_and(odd, has_next))
    def _():
        greet((ahead, g))

    @pl.when(first)
    def _():
        pl.semaphore_wait(barrier, 5)

    @pl.when(jnp.logical_and(even, p > 0))
    def _():
        pl.semaphore_wait(barrier, 6)

    @pl.when(jnp.logical_and(odd, has_next))
    def _():
        pl.semaphore_wait(barrier, 4)

    @pl.when(p == sections - 1)
    def _():
        pl.semaphore_wait(barrier, 3)

    def picked(block, m, side):
        chosen = ids_ref[m, side, 0, g]
        return jnp.where(chosen == 0, block[:edge], block[edge:])

    def forward(m, pieces=range(chunks)):
        for c in pieces:

            @pl.when(first)
            def _():
                load_features(m, c).wait()

            @pl.when(p > 0)
            def _():
                send_own(m, c).wait_recv()

            block = own[m, c]
            for side in range(2):
                fwd_stage[m, side, c] = picked(block, m, side)
                send_forward(m, side, c).start()

    @pl.when(first)
    def _():
        forward(0)

    load_tiles.wait()

    def build_table(m, carry):
        for d in range(rows // edge):
            for s in range(slots):
                total = jnp.zeros((edge, edge), jnp.float32)
                for t in range(tile_count):
                    here = jnp.logical_and(coords_ref[m, 0, t] == d, coords_ref[m, 1, t] == s)
                    total += tiles[m, t].astype(jnp.float32) * jnp.where(here, 1.0, 0.0)
                table[m, pl.ds(d * edge, edge), pl.ds(s * edge, edge)] = total.astype(jnp.bfloat16)
        return carry

    lax.fori_loop(0, micro_count, build_table, 0)
    load_weight.wait()
    load_gain.wait()

    @pl.when(jnp.logical_and(even, p > 0))
    def _():
        forward(0)

    def micro_step(m, carry):
        @pl.when(jnp.logical_and(even, m < micro_count - 1))
        def _():
            forward(m + 1, range(chunks - 1))

        for c in range(chunks):

            @pl.when(odd)
            def _():
                send_own(m, c).wait_recv()

            agg = jnp.dot(
                table[m, :, :rows], own[m, c], preferred_element_type=jnp.float32
            )
            for side in range(2):
                send_forward(m, side, c).wait_recv()
                agg += jnp.dot(
                    table[m, :, pl.ds(rows + side * edge, edge)],
                    halo[m, side, c],
                    preferred_element_type=jnp.float32,
                )
            part = jnp.dot(
                agg.astype(jnp.bfloat16),
                weight[pl.ds(c * cols, cols), :],
                preferred_element_type=jnp.float32,
            )
            if c == 0:
                z_acc[...] = part
            elif c < chunks - 1:
                z_acc[...] += part
            else:
                act = jnp.maximum(z_acc[...] + part, 0.0)
        scale = 1.0 / jnp.sqrt(jnp.mean(act * act, axis=-1, keepdims=True) + 1e-06)
        for c in range(chunks):
            block = act[:, c * cols : (c + 1) * cols] * scale
            block = (block * gain_ref[:, pl.ds(c * cols, cols)]).astype(jnp.bfloat16)
            result[m, c] = block
            for side in range(2):
                halo_stage[m, side, c] = picked(block, m, side)

        @pl.when(jnp.logical_and(even, m < micro_count - 1))
        def _():
            forward(m + 1, range(chunks - 1, chunks))

        @pl.when(even)
        def _():
            for c in range(chunks):
                for side in range(2):
                    send_halo(m, side, c).start()

        @pl.when(has_next)
        def _():
            for c in range(chunks):
                send_own(m, c).start()

        for c in range(chunks):
            save(m, c).start()
        return carry

    lax.fori_loop(0, micro_count, micro_step, 0)

    def finish(m, carry):
        for c in range(chunks):
            save(m, c).wait()

            @pl.when(has_next)
            def _():
                send_own(m, c).wait_send()

            @pl.when(even)
            def _():
                for side in range(2):
                    send_forward(m, side, c).wait_send()
                    send_halo(m, side, c).wait_send()

        return carry

    lax.fori_loop(0, micro_count, finish, 0)


def on_device(features, weights, gains, tiles, tile_coords, send_ids):
    micro_count, rows, width = features.shape
    tile_count, edge = tiles.shape[1], tiles.shape[-1]
    slots = rows // edge + 2
    cols = width // CHUNKS
    per_chunk = (micro_count, CHUNKS)
    per_side = (micro_count, 2, CHUNKS)
    result = pl.pallas_call(
        functools.partial(kernel, lax.axis_size("pipe"), lax.axis_size("graph")),
        out_shape=jax.ShapeDtypeStruct((micro_count, rows, width), jnp.bfloat16),
        in_specs=[
            pl.BlockSpec(memory_space=pltpu.SMEM),
            pl.BlockSpec(memory_space=pltpu.SMEM),
            pl.BlockSpec(memory_space=pltpu.HBM),
            pl.BlockSpec(memory_space=pltpu.HBM),
            pl.BlockSpec(memory_space=pltpu.HBM),
            pl.BlockSpec(memory_space=pltpu.HBM),
        ],
        out_specs=pl.BlockSpec(memory_space=pl.ANY),
        scratch_shapes=[
            pltpu.VMEM(per_chunk + (rows, cols), jnp.bfloat16),
            pltpu.VMEM(per_side + (edge, cols), jnp.bfloat16),
            pltpu.VMEM(per_side + (edge, cols), jnp.bfloat16),
            pltpu.VMEM(per_side + (edge, cols), jnp.bfloat16),
            pltpu.VMEM(per_chunk + (rows, cols), jnp.bfloat16),
            pltpu.VMEM((width, width), jnp.bfloat16),
            pltpu.VMEM((1, width), jnp.float32),
            pltpu.VMEM((micro_count, tile_count, edge, edge), jnp.bfloat16),
            pltpu.VMEM((micro_count, rows, slots * edge), jnp.bfloat16),
            pltpu.VMEM((rows, width), jnp.float32),
            pltpu.SemaphoreType.DMA(per_chunk),
            pltpu.SemaphoreType.DMA(per_chunk),
            pltpu.SemaphoreType.DMA(per_side),
            pltpu.SemaphoreType.DMA(per_side),
            pltpu.SemaphoreType.DMA(per_side),
            pltpu.SemaphoreType.DMA(per_chunk),
            pltpu.SemaphoreType.DMA(per_chunk),
            pltpu.SemaphoreType.DMA((3,)),
        ],
        compiler_params=pltpu.CompilerParams(
            collective_id=0, has_side_effects=True, vmem_limit_bytes=60 * 1024 * 1024
        ),
    )(
        jnp.transpose(send_ids, (0, 2, 3, 1)),
        jnp.transpose(tile_coords, (0, 2, 1)),
        gains,
        features,
        weights[0],
        tiles,
    )
    return result[None]


def solution(mesh):
    placed = (
        P(None, "graph", None),
        P("pipe", None, None),
        P("pipe", None),
        P(None, "graph", None, None),
        P(None, "graph", None),
        P(),
    )
    return jax.shard_map(
        on_device,
        mesh=mesh,
        in_specs=placed,
        out_specs=P("pipe", None, "graph", None),
        check_vma=False,
    )
```

```python
import functools

import jax
import jax.numpy as jnp
from jax import lax
from jax.experimental import pallas as pl
from jax.experimental.pallas import tpu as pltpu
from jax.sharding import PartitionSpec as P

MESH = pl.DeviceIdType.MESH
CHUNKS = 4


def kernel(
    sections,
    partitions,
    ids_ref,
    coords_ref,
    gain_hbm,
    features_ref,
    weight_hbm,
    tiles_hbm,
    out_hbm,
    own,
    halo,
    fwd_stage,
    halo_stage,
    result,
    weight,
    gain_ref,
    tiles,
    table,
    z_acc,
    own_send,
    own_recv,
    fwd_send,
    halo_send,
    halo_recv,
    feature_sem,
    out_sem,
    load_sem,
):
    p = lax.axis_index("pipe")
    g = lax.axis_index("graph")
    right = lax.rem(g + 1, partitions)
    left = lax.rem(g + partitions - 1, partitions)
    micro_count, chunks, rows, cols = own.shape
    edge = halo.shape[3]
    tile_count = tiles.shape[1]
    slots = rows // edge + 2
    even = lax.rem(p, 2) == 0
    odd = jnp.logical_not(even)
    first = p == 0
    has_next = p < sections - 1
    ahead = jnp.minimum(p + 1, sections - 1)
    behind = jnp.maximum(p - 1, 0)

    load_weight = pltpu.make_async_copy(weight_hbm, weight, load_sem.at[0])
    load_gain = pltpu.make_async_copy(gain_hbm, gain_ref, load_sem.at[2])
    load_tiles = pltpu.make_async_copy(tiles_hbm, tiles, load_sem.at[1])

    def load_features(m, c):
        return pltpu.make_async_copy(
            features_ref.at[m, :, pl.ds(c * cols, cols)], own.at[m, c], feature_sem.at[m, c]
        )

    def send_own(m, c):
        return pltpu.make_async_remote_copy(
            src_ref=result.at[m, c],
            dst_ref=own.at[m, c],
            send_sem=own_send.at[m, c],
            recv_sem=own_recv.at[m, c],
            device_id=(ahead, g),
            device_id_type=MESH,
        )

    def send_forward(m, side, c):
        return pltpu.make_async_remote_copy(
            src_ref=fwd_stage.at[m, side, c],
            dst_ref=halo.at[m, side, c],
            send_sem=fwd_send.at[m, side, c],
            recv_sem=halo_recv.at[m, side, c],
            device_id=(p, left if side else right),
            device_id_type=MESH,
        )

    def send_halo(m, side, c):
        return pltpu.make_async_remote_copy(
            src_ref=halo_stage.at[m, side, c],
            dst_ref=halo.at[m, side, c],
            send_sem=halo_send.at[m, side, c],
            recv_sem=halo_recv.at[m, side, c],
            device_id=(ahead, left if side else right),
            device_id_type=MESH,
        )

    def save(m, c):
        return pltpu.make_async_copy(
            result.at[m, c], out_hbm.at[m, :, pl.ds(c * cols, cols)], out_sem.at[m, c]
        )

    load_tiles.start()
    load_weight.start()
    load_gain.start()

    @pl.when(first)
    def _():
        for m in range(micro_count):
            for c in range(chunks):
                load_features(m, c).start()

    barrier = pltpu.get_barrier_semaphore()

    def greet(*where):
        for device in where:
            pl.semaphore_signal(barrier, inc=1, device_id=device, device_id_type=MESH)

    @pl.when(even)
    def _():
        greet((p, right), (p, left), (ahead, g), (ahead, right), (ahead, left))

    @pl.when(odd)
    def _():
        greet((behind, g), (behind, right), (behind, left))

    @pl.when(jnp.logical_and(even, p > 0))
    def _():
        greet((behind, g))

    @pl.when(jnp.logical_and(odd, has_next))
    def _():
        greet((ahead, g))

    @pl.when(first)
    def _():
        pl.semaphore_wait(barrier, 5)

    @pl.when(jnp.logical_and(even, p > 0))
    def _():
        pl.semaphore_wait(barrier, 6)

    @pl.when(jnp.logical_and(odd, has_next))
    def _():
        pl.semaphore_wait(barrier, 4)

    @pl.when(p == sections - 1)
    def _():
        pl.semaphore_wait(barrier, 3)

    def picked(block, m, side):
        chosen = ids_ref[m, side, 0, g]
        return jnp.where(chosen == 0, block[:edge], block[edge:])

    def forward(m, pieces=range(chunks)):
        for c in pieces:

            @pl.when(first)
            def _():
                load_features(m, c).wait()

            @pl.when(p > 0)
            def _():
                send_own(m, c).wait_recv()

            block = own[m, c]
            for side in range(2):
                fwd_stage[m, side, c] = picked(block, m, side)
                send_forward(m, side, c).start()

    @pl.when(first)
    def _():
        forward(0)

    load_tiles.wait()

    def build_table(m, carry):
        for d in range(rows // edge):
            for s in range(slots):
                total = jnp.zeros((edge, edge), jnp.float32)
                for t in range(tile_count):
                    here = jnp.logical_and(coords_ref[m, 0, t] == d, coords_ref[m, 1, t] == s)
                    total += tiles[m, t].astype(jnp.float32) * jnp.where(here, 1.0, 0.0)
                table[m, pl.ds(d * edge, edge), pl.ds(s * edge, edge)] = total.astype(jnp.bfloat16)
        return carry

    lax.fori_loop(0, micro_count, build_table, 0)
    load_weight.wait()
    load_gain.wait()

    @pl.when(jnp.logical_and(even, p > 0))
    def _():
        forward(0)

    def micro_step(m, carry):
        @pl.when(jnp.logical_and(even, m < micro_count - 1))
        def _():
            forward(m + 1, range(chunks - 1))

        for c in range(chunks):

            @pl.when(odd)
            def _():
                send_own(m, c).wait_recv()

            for side in range(2):
                send_forward(m, side, c).wait_recv()
            agg = jnp.dot(
                table[m, :, pl.ds(0, rows)], own[m, c], preferred_element_type=jnp.float32
            )
            agg += jnp.dot(
                table[m, :, pl.ds(rows, 2 * edge)],
                halo[m, :, c].reshape(2 * edge, cols),
                preferred_element_type=jnp.float32,
            )
            if c == 0:
                head = agg.astype(jnp.bfloat16)
                continue
            if c == 1:
                agg = jnp.concatenate([head, agg.astype(jnp.bfloat16)], axis=1)
            part = jnp.dot(
                agg.astype(jnp.bfloat16),
                weight[pl.ds((c + 1) * cols - agg.shape[1], agg.shape[1]), :],
                preferred_element_type=jnp.float32,
            )
            if c == 1:
                z_acc[...] = part
            elif c < chunks - 1:
                z_acc[...] += part
            else:
                act = jnp.maximum(z_acc[...] + part, 0.0)
        scale = 1.0 / jnp.sqrt(jnp.mean(act * act, axis=-1, keepdims=True) + 1e-06)
        for c in range(chunks):
            block = act[:, c * cols : (c + 1) * cols] * scale
            block = (block * gain_ref[:, pl.ds(c * cols, cols)]).astype(jnp.bfloat16)
            result[m, c] = block
            for side in range(2):
                halo_stage[m, side, c] = picked(block, m, side)

        @pl.when(jnp.logical_and(even, m < micro_count - 1))
        def _():
            forward(m + 1, range(chunks - 1, chunks))

        @pl.when(even)
        def _():
            for c in range(chunks):
                for side in range(2):
                    send_halo(m, side, c).start()

        @pl.when(has_next)
        def _():
            for c in range(chunks):
                send_own(m, c).start()

        for c in range(chunks):
            save(m, c).start()
        return carry

    lax.fori_loop(0, micro_count, micro_step, 0)

    def finish(m, carry):
        for c in range(chunks):
            save(m, c).wait()

            @pl.when(has_next)
            def _():
                send_own(m, c).wait_send()

            @pl.when(even)
            def _():
                for side in range(2):
                    send_forward(m, side, c).wait_send()
                    send_halo(m, side, c).wait_send()

        return carry

    lax.fori_loop(0, micro_count, finish, 0)


def on_device(features, weights, gains, tiles, tile_coords, send_ids):
    micro_count, rows, width = features.shape
    tile_count, edge = tiles.shape[1], tiles.shape[-1]
    slots = rows // edge + 2
    cols = width // CHUNKS
    per_chunk = (micro_count, CHUNKS)
    per_side = (micro_count, 2, CHUNKS)
    result = pl.pallas_call(
        functools.partial(kernel, lax.axis_size("pipe"), lax.axis_size("graph")),
        out_shape=jax.ShapeDtypeStruct((micro_count, rows, width), jnp.bfloat16),
        in_specs=[
            pl.BlockSpec(memory_space=pltpu.SMEM),
            pl.BlockSpec(memory_space=pltpu.SMEM),
            pl.BlockSpec(memory_space=pltpu.HBM),
            pl.BlockSpec(memory_space=pltpu.HBM),
            pl.BlockSpec(memory_space=pltpu.HBM),
            pl.BlockSpec(memory_space=pltpu.HBM),
        ],
        out_specs=pl.BlockSpec(memory_space=pl.ANY),
        scratch_shapes=[
            pltpu.VMEM(per_chunk + (rows, cols), jnp.bfloat16),
            pltpu.VMEM(per_side + (edge, cols), jnp.bfloat16),
            pltpu.VMEM(per_side + (edge, cols), jnp.bfloat16),
            pltpu.VMEM(per_side + (edge, cols), jnp.bfloat16),
            pltpu.VMEM(per_chunk + (rows, cols), jnp.bfloat16),
            pltpu.VMEM((width, width), jnp.bfloat16),
            pltpu.VMEM((1, width), jnp.float32),
            pltpu.VMEM((micro_count, tile_count, edge, edge), jnp.bfloat16),
            pltpu.VMEM((micro_count, rows, slots * edge), jnp.bfloat16),
            pltpu.VMEM((rows, width), jnp.float32),
            pltpu.SemaphoreType.DMA(per_chunk),
            pltpu.SemaphoreType.DMA(per_chunk),
            pltpu.SemaphoreType.DMA(per_side),
            pltpu.SemaphoreType.DMA(per_side),
            pltpu.SemaphoreType.DMA(per_side),
            pltpu.SemaphoreType.DMA(per_chunk),
            pltpu.SemaphoreType.DMA(per_chunk),
            pltpu.SemaphoreType.DMA((3,)),
        ],
        compiler_params=pltpu.CompilerParams(
            collective_id=0, has_side_effects=True, vmem_limit_bytes=60 * 1024 * 1024
        ),
    )(
        jnp.transpose(send_ids, (0, 2, 3, 1)),
        jnp.transpose(tile_coords, (0, 2, 1)),
        gains,
        features,
        weights[0],
        tiles,
    )
    return result[None]


def solution(mesh):
    placed = (
        P(None, "graph", None),
        P("pipe", None, None),
        P("pipe", None),
        P(None, "graph", None, None),
        P(None, "graph", None),
        P(),
    )
    return jax.shard_map(
        on_device,
        mesh=mesh,
        in_specs=placed,
        out_specs=P("pipe", None, "graph", None),
        check_vma=False,
    )
```

```python
import functools

import jax
import jax.numpy as jnp
from jax import lax
from jax.experimental import pallas as pl
from jax.experimental.pallas import tpu as pltpu
from jax.sharding import PartitionSpec as P

MESH = pl.DeviceIdType.MESH
CHUNKS = 4


def kernel(
    sections,
    partitions,
    ids_ref,
    coords_ref,
    gain_hbm,
    features_ref,
    weight_hbm,
    tiles_hbm,
    out_hbm,
    own,
    halo,
    fwd_stage,
    halo_stage,
    result,
    weight,
    gain_ref,
    tiles,
    table,
    z_acc,
    own_send,
    own_recv,
    fwd_send,
    halo_send,
    halo_recv,
    feature_sem,
    out_sem,
    load_sem,
):
    p = lax.axis_index("pipe")
    g = lax.axis_index("graph")
    right = lax.rem(g + 1, partitions)
    left = lax.rem(g + partitions - 1, partitions)
    micro_count, chunks, rows, cols = own.shape
    edge = halo.shape[3]
    tile_count = tiles.shape[1]
    slots = rows // edge + 2
    even = lax.rem(p, 2) == 0
    odd = jnp.logical_not(even)
    first = p == 0
    has_next = p < sections - 1
    ahead = jnp.minimum(p + 1, sections - 1)
    behind = jnp.maximum(p - 1, 0)

    load_weight = pltpu.make_async_copy(weight_hbm, weight, load_sem.at[0])
    load_gain = pltpu.make_async_copy(gain_hbm, gain_ref, load_sem.at[2])
    load_tiles = pltpu.make_async_copy(tiles_hbm, tiles, load_sem.at[1])

    def load_features(m, c):
        return pltpu.make_async_copy(
            features_ref.at[m, :, pl.ds(c * cols, cols)], own.at[m, c], feature_sem.at[m, c]
        )

    def send_own(m, c):
        return pltpu.make_async_remote_copy(
            src_ref=result.at[m, c],
            dst_ref=own.at[m, c],
            send_sem=own_send.at[m, c],
            recv_sem=own_recv.at[m, c],
            device_id=(ahead, g),
            device_id_type=MESH,
        )

    def send_forward(m, side, c):
        return pltpu.make_async_remote_copy(
            src_ref=fwd_stage.at[m, side, c],
            dst_ref=halo.at[m, side, c],
            send_sem=fwd_send.at[m, side, c],
            recv_sem=halo_recv.at[m, side, c],
            device_id=(p, left if side else right),
            device_id_type=MESH,
        )

    def send_halo(m, side, c):
        return pltpu.make_async_remote_copy(
            src_ref=halo_stage.at[m, side, c],
            dst_ref=halo.at[m, side, c],
            send_sem=halo_send.at[m, side, c],
            recv_sem=halo_recv.at[m, side, c],
            device_id=(ahead, left if side else right),
            device_id_type=MESH,
        )

    def save(m, c):
        return pltpu.make_async_copy(
            result.at[m, c], out_hbm.at[m, :, pl.ds(c * cols, cols)], out_sem.at[m, c]
        )

    load_tiles.start()
    load_weight.start()
    load_gain.start()

    @pl.when(first)
    def _():
        for m in range(micro_count):
            for c in range(chunks):
                load_features(m, c).start()

    barrier = pltpu.get_barrier_semaphore()

    def greet(*where):
        for device in where:
            pl.semaphore_signal(barrier, inc=1, device_id=device, device_id_type=MESH)

    @pl.when(even)
    def _():
        greet((p, right), (p, left), (ahead, g), (ahead, right), (ahead, left))

    @pl.when(odd)
    def _():
        greet((behind, g), (behind, right), (behind, left))

    @pl.when(jnp.logical_and(even, p > 0))
    def _():
        greet((behind, g))

    @pl.when(jnp.logical_and(odd, has_next))
    def _():
        greet((ahead, g))

    @pl.when(first)
    def _():
        pl.semaphore_wait(barrier, 5)

    @pl.when(jnp.logical_and(even, p > 0))
    def _():
        pl.semaphore_wait(barrier, 6)

    @pl.when(jnp.logical_and(odd, has_next))
    def _():
        pl.semaphore_wait(barrier, 4)

    @pl.when(p == sections - 1)
    def _():
        pl.semaphore_wait(barrier, 3)

    def picked(block, m, side):
        chosen = ids_ref[m, side, 0, g]
        return jnp.where(chosen == 0, block[:edge], block[edge:])

    def forward(m, pieces=range(chunks)):
        for c in pieces:

            @pl.when(first)
            def _():
                load_features(m, c).wait()

            @pl.when(p > 0)
            def _():
                send_own(m, c).wait_recv()

            block = own[m, c]
            for side in range(2):
                fwd_stage[m, side, c] = picked(block, m, side)
                send_forward(m, side, c).start()

    @pl.when(first)
    def _():
        forward(0)

    load_tiles.wait()

    def build_table(m, carry):
        for d in range(rows // edge):
            for s in range(slots):
                total = jnp.zeros((edge, edge), jnp.float32)
                for t in range(tile_count):
                    here = jnp.logical_and(coords_ref[m, 0, t] == d, coords_ref[m, 1, t] == s)
                    total += tiles[m, t].astype(jnp.float32) * jnp.where(here, 1.0, 0.0)
                table[m, pl.ds(d * edge, edge), pl.ds(s * edge, edge)] = total.astype(jnp.bfloat16)
        return carry

    lax.fori_loop(0, micro_count, build_table, 0)
    load_weight.wait()
    load_gain.wait()

    @pl.when(jnp.logical_and(even, p > 0))
    def _():
        forward(0)

    def micro_step(m, carry):
        @pl.when(jnp.logical_and(even, m < micro_count - 1))
        def _():
            forward(m + 1, range(chunks - 1))

        for c in range(chunks):

            @pl.when(odd)
            def _():
                send_own(m, c).wait_recv()

            for side in range(2):
                send_forward(m, side, c).wait_recv()
            agg = jnp.dot(
                table[m, :, pl.ds(0, rows)], own[m, c], preferred_element_type=jnp.float32
            )
            agg += jnp.dot(
                table[m, :, pl.ds(rows, 2 * edge)],
                halo[m, :, c].reshape(2 * edge, cols),
                preferred_element_type=jnp.float32,
            )
            if c == 0:
                head = agg.astype(jnp.bfloat16)
                continue
            if c == 1:
                agg = jnp.concatenate([head, agg.astype(jnp.bfloat16)], axis=1)
            part = jnp.dot(
                agg.astype(jnp.bfloat16),
                weight[pl.ds((c + 1) * cols - agg.shape[1], agg.shape[1]), :],
                preferred_element_type=jnp.float32,
            )
            if c == 1:
                z_acc[...] = part
            elif c < chunks - 1:
                z_acc[...] += part
            else:
                act = jnp.maximum(z_acc[...] + part, 0.0)
        scale = 1.0 / jnp.sqrt(jnp.mean(act * act, axis=-1, keepdims=True) + 1e-06)
        for c in range(chunks):
            block = act[:, c * cols : (c + 1) * cols] * scale
            block = (block * gain_ref[:, pl.ds(c * cols, cols)]).astype(jnp.bfloat16)
            result[m, c] = block

        @pl.when(jnp.logical_and(even, m < micro_count - 1))
        def _():
            forward(m + 1, range(chunks - 1, chunks))

        @pl.when(even)
        def _():
            for c in range(chunks):
                for side in range(2):
                    halo_stage[m, side, c] = picked(result[m, c], m, side)
                    send_halo(m, side, c).start()

        @pl.when(has_next)
        def _():
            for c in range(chunks):
                send_own(m, c).start()

        for c in range(chunks):
            save(m, c).start()
        return carry

    lax.fori_loop(0, micro_count, micro_step, 0)

    def finish(m, carry):
        for c in range(chunks):
            save(m, c).wait()

            @pl.when(has_next)
            def _():
                send_own(m, c).wait_send()

            @pl.when(even)
            def _():
                for side in range(2):
                    send_forward(m, side, c).wait_send()
                    send_halo(m, side, c).wait_send()

        return carry

    lax.fori_loop(0, micro_count, finish, 0)


def on_device(features, weights, gains, tiles, tile_coords, send_ids):
    micro_count, rows, width = features.shape
    tile_count, edge = tiles.shape[1], tiles.shape[-1]
    slots = rows // edge + 2
    cols = width // CHUNKS
    per_chunk = (micro_count, CHUNKS)
    per_side = (micro_count, 2, CHUNKS)
    result = pl.pallas_call(
        functools.partial(kernel, lax.axis_size("pipe"), lax.axis_size("graph")),
        out_shape=jax.ShapeDtypeStruct((micro_count, rows, width), jnp.bfloat16),
        in_specs=[
            pl.BlockSpec(memory_space=pltpu.SMEM),
            pl.BlockSpec(memory_space=pltpu.SMEM),
            pl.BlockSpec(memory_space=pltpu.HBM),
            pl.BlockSpec(memory_space=pltpu.HBM),
            pl.BlockSpec(memory_space=pltpu.HBM),
            pl.BlockSpec(memory_space=pltpu.HBM),
        ],
        out_specs=pl.BlockSpec(memory_space=pl.ANY),
        scratch_shapes=[
            pltpu.VMEM(per_chunk + (rows, cols), jnp.bfloat16),
            pltpu.VMEM(per_side + (edge, cols), jnp.bfloat16),
            pltpu.VMEM(per_side + (edge, cols), jnp.bfloat16),
            pltpu.VMEM(per_side + (edge, cols), jnp.bfloat16),
            pltpu.VMEM(per_chunk + (rows, cols), jnp.bfloat16),
            pltpu.VMEM((width, width), jnp.bfloat16),
            pltpu.VMEM((1, width), jnp.float32),
            pltpu.VMEM((micro_count, tile_count, edge, edge), jnp.bfloat16),
            pltpu.VMEM((micro_count, rows, slots * edge), jnp.bfloat16),
            pltpu.VMEM((rows, width), jnp.float32),
            pltpu.SemaphoreType.DMA(per_chunk),
            pltpu.SemaphoreType.DMA(per_chunk),
            pltpu.SemaphoreType.DMA(per_side),
            pltpu.SemaphoreType.DMA(per_side),
            pltpu.SemaphoreType.DMA(per_side),
            pltpu.SemaphoreType.DMA(per_chunk),
            pltpu.SemaphoreType.DMA(per_chunk),
            pltpu.SemaphoreType.DMA((3,)),
        ],
        compiler_params=pltpu.CompilerParams(
            collective_id=0, has_side_effects=True, vmem_limit_bytes=60 * 1024 * 1024
        ),
    )(
        jnp.transpose(send_ids, (0, 2, 3, 1)),
        jnp.transpose(tile_coords, (0, 2, 1)),
        gains,
        features,
        weights[0],
        tiles,
    )
    return result[None]


def solution(mesh):
    placed = (
        P(None, "graph", None),
        P("pipe", None, None),
        P("pipe", None),
        P(None, "graph", None, None),
        P(None, "graph", None),
        P(),
    )
    return jax.shard_map(
        on_device,
        mesh=mesh,
        in_specs=placed,
        out_specs=P("pipe", None, "graph", None),
        check_vma=False,
    )
```
